32 devices in a mesh: grp: 2 (over y), rad: 8 (over z, x), orb: 2 (over core).
Axes of the slice: x: 2, y: 2, z: 4, core: 2. Of those that a mesh axis runs over, the one named last changes fastest.
Arguments:
- occupied: bfloat16 [32, 2, 16, 3470], P('orb', None, 'rad'), may hold values from -6 to 6
- continuum: bfloat16 [2, 32, 3470], P(None, ('grp', 'rad')), parts along dimension 1, may hold values from -6 to 6
- harmonics: bfloat16 [3470, 961], P('orb'), may hold values from -1.6953125 to 1.6953125
- angle_weight: float32 [3470], replicated, may hold values from 0.0018 to 0.0072
- radial_weight: float32 [16], P('rad'), may hold values from 0.005 to 0.04
- radius: float32 [16], P('rad'), may hold values from 1 to 4, as said below
- harmonic_order: int32 [961], replicated, may hold values from 0 to 960, each once
Outputs:
- exchange_field: float32 [2, 32, 3470], P(None, ('grp', 'rad'), 'orb'), parts along dimension 1
The draws below stay inside these ranges and needn't reach their ends.
There are 2 independent parts, one for each index of `grp`. The reference program is written for one: setup_inputs(seed, part) draws one part's arguments, and reference() takes and returns one part's arrays. A program takes and returns all parts, laid end to end along the dimension named above; an argument that names none is the same for every part. Nothing has to cross between parts.
Inputs may be any that keep to these rules, and one draw needn't show every extreme that they name: `radius`: radii increase strictly with the radial index.
All inputs are finite; a program needn't handle non-finite values.
Results may differ from the reference program's by a relative error of at most 0.0032.
Values may be sent and summed in bfloat16 or wider, within the bound.
A program may use at most 128 MiB of HBM per device.

```python
import math
import jax
import jax.numpy as jnp
from jax import lax

NORB = 32
LMAX = 30
LM = 961
NP = 3470
NR = 16


def draw_radius(key, part):
    position = jnp.arange(NR).astype(jnp.float32)
    jitter = jax.random.uniform(key, (NR,), jnp.float32, 0.1, 0.8)
    return 1.0 + 3.0 * (position + jitter) / NR


def levels(rng, shape, split, least, top_value):
    level, own = 1.0, jax.random.fold_in(rng, 6)
    for dim, parts in split:
        heights = jnp.exp(jax.random.uniform(jax.random.fold_in(own, dim), (parts,), jnp.float32, least / len(split), top_value / len(split)))
        level = level * jnp.repeat(heights, shape[dim] // parts).reshape([-1 if axis == dim else 1 for axis in range(len(shape))])
    return level


def scatter_about(rng, dims, width, bound, split=(), held_as=jnp.bfloat16):
    array = width * jax.random.normal(rng, dims, jnp.float32)
    if split:
        array = array * levels(rng, dims, split, -0.22, 0.18)
    return jnp.clip(array, -bound, bound).astype(held_as)


def setup_inputs(seed: int = 0, part: int = 0) -> dict:
    seeds = jax.random.split(jax.random.key(seed), 8)
    own_keys = jax.random.split(jax.random.fold_in(seeds[7], part), 8)
    return {
        "occupied": scatter_about(seeds[0], (NORB, 2, NR, NP), 1.0, 6.0, ((0, 2), (2, 8))),
        "continuum": scatter_about(own_keys[1], (2, NR, NP), 1.0, 6.0, ((1, 8),)),
        "harmonics": scatter_about(seeds[2], (NP, LM), 0.28, 1.6953125, ((0, 2),)),
        "angle_weight": jnp.clip(jnp.exp(jax.random.uniform(seeds[3], (NP,), jnp.float32, math.log(0.0018), math.log(0.0072))), 0.0018, 0.0072),
        "radial_weight": jnp.clip(jnp.exp(math.log(0.04) - 2.0794415 * jax.random.uniform(seeds[4], (NR,), jnp.float32) ** levels(seeds[4], (NR,), ((0, 8),), -0.2, 0.2)), 0.005, 0.04),
        "radius": draw_radius(jax.random.fold_in(seeds[7], 71), part),
        "harmonic_order": jax.random.permutation(seeds[6], LM).astype(jnp.int32),
    }


FOUR_PI = 12.566370614359172


def degree_of(harmonic_order):
    squares = (jnp.arange(1, LMAX + 1) ** 2).astype(jnp.int32)
    hits = (harmonic_order[:, None] >= squares[None, :]).astype(jnp.int32)
    return jnp.sum(hits, axis=1).astype(jnp.int32)


def pair_density(occupied, continuum, angle_weight):
    occ_real = occupied[:, 0].astype(jnp.float32)
    occ_imag = occupied[:, 1].astype(jnp.float32)
    cont_real = continuum[0].astype(jnp.float32)[None]
    cont_imag = continuum[1].astype(jnp.float32)[None]
    real_part = (occ_real * cont_real + occ_imag * cont_imag) * angle_weight
    imag_part = (occ_real * cont_imag - occ_imag * cont_real) * angle_weight
    return jnp.stack([real_part, imag_part], axis=1).astype(jnp.bfloat16)


def combine_field(occupied, grid_values):
    occ_real = occupied[:, 0].astype(jnp.float32)
    occ_imag = occupied[:, 1].astype(jnp.float32)
    real_part = jnp.sum(occ_real * grid_values[:, 0] - occ_imag * grid_values[:, 1], axis=0)
    imag_part = jnp.sum(occ_real * grid_values[:, 1] + occ_imag * grid_values[:, 0], axis=0)
    return jnp.stack([real_part, imag_part], axis=0)


def reference(occupied, continuum, harmonics, angle_weight, radial_weight, radius, harmonic_order):
    degree = degree_of(harmonic_order).astype(jnp.float32)
    factor = FOUR_PI / (2.0 * degree + 1.0)

    def one_orbital(running_sum, orbital):
        density = pair_density(orbital[None], continuum, angle_weight)[0]
        moments = jnp.dot(density.reshape(2 * NR, NP), harmonics, preferred_element_type=jnp.float32)
        charge = moments.reshape(2, NR, LM) * radial_weight[None, :, None]
        charge_rows = jnp.transpose(charge, (1, 0, 2))

        def advance_inner(carried, inputs):
            accum_total, anchor = carried
            row_charge, row_radius = inputs
            accum_total = jnp.power(anchor / row_radius, degree) * accum_total + row_charge
            return (accum_total, row_radius), accum_total

        start_state = (jnp.zeros_like(charge_rows[0]), radius[0])
        first_state, inner_rows = lax.scan(advance_inner, start_state, (charge_rows, radius))

        def advance_outer(carried, inputs):
            accum_total, anchor = carried
            row_charge, row_radius = inputs
            outer_row = jnp.power(row_radius / anchor, degree) * accum_total
            return (outer_row + row_charge / row_radius, row_radius), outer_row

        end_state = (jnp.zeros_like(charge_rows[0]), radius[NR - 1])
        last_state, outer_rows = lax.scan(advance_outer, end_state, (charge_rows, radius), reverse=True)
        potential = factor * (inner_rows / radius[:, None, None] + outer_rows)
        potential = jnp.transpose(potential, (1, 0, 2)).astype(jnp.bfloat16)
        grid_values = lax.dot_general(potential.reshape(2 * NR, LM), harmonics, (((1,), (1,)), ((), ())), preferred_element_type=jnp.float32)
        grid_values = grid_values.reshape(1, 2, NR, NP)
        return running_sum + combine_field(orbital[None], grid_values), None

    total_field, ignored = lax.scan(one_orbital, jnp.zeros((2, NR, NP), jnp.float32), occupied)
    return total_field
```

```python
import functools

import jax
import jax.numpy as jnp
from jax import lax
from jax.experimental import pallas as pl
from jax.experimental.pallas import tpu as pltpu
from jax.sharding import PartitionSpec as P

LMAX = 30
FOUR_PI = 12.566370614359172
MESH = pl.DeviceIdType.MESH
LANES = 128
CHUNK = 256
F32 = jnp.float32
BF16 = jnp.bfloat16


def degree_of(harmonic_order):
    squares = (jnp.arange(1, LMAX + 1) ** 2).astype(jnp.int32)
    hits = (harmonic_order[:, None] >= squares[None, :]).astype(jnp.int32)
    return jnp.sum(hits, axis=1)


def kernel(
    n_rad, io, points, modes,
    occ_ref, cont_ref, degree_ref, radius_ref, weight_ref, table_hbm, out_ref,
    table, occ_in, occ, cont, dens, m_own, m_send, m_recv, st, inbox, carried, carry, pot,
    table_sem, sib_send, sib_recv, m_send_sem, m_recv_sem, up_send, up_recv, back_send, back_recv,
):
    me, core = lax.axis_index("rad"), lax.axis_index("orb")
    sibling = 1 - core
    rows = 4 * io
    half = 2 * io
    units = st.shape[0]
    stride = n_rad // units
    wide = occ.shape[2]
    window = occ_in.shape[1]
    base = points // LANES * LANES
    shift = points - base
    chunks = m_own.shape[0]

    fetch = pltpu.make_async_copy(table_hbm, table, table_sem)
    fetch.start()

    barrier = pltpu.get_barrier_semaphore()
    pl.semaphore_signal(barrier, inc=1, device_id={"orb": sibling}, device_id_type=MESH)

    def greet(step, carry_in):
        other = lax.rem(me + step, n_rad)
        pl.semaphore_signal(barrier, inc=1, device_id={"rad": other}, device_id_type=MESH)
        return carry_in

    lax.fori_loop(1, n_rad, greet, 0)
    pl.semaphore_wait(barrier, n_rad)

    send_occ = pltpu.make_async_remote_copy(
        src_ref=occ_ref.at[:, pl.ds(pl.multiple_of(sibling * base, LANES), window)],
        dst_ref=occ_in,
        send_sem=sib_send.at[0],
        recv_sem=sib_recv.at[0],
        device_id={"orb": sibling},
        device_id_type=MESH,
    )
    send_occ.start()

    degree = degree_ref[...]
    r0, r1, w0, w1 = radius_ref[0], radius_ref[1], weight_ref[0], weight_ref[1]
    log0 = jnp.log(jnp.full(degree.shape, r0, F32))
    log1 = jnp.log(jnp.full(degree.shape, r1, F32))
    up0, up1 = jnp.exp(degree * log0), jnp.exp(degree * log1)
    down0, down1 = jnp.exp(-degree * log0), jnp.exp(-degree * log1)
    a0, a1 = up0 * w0, up1 * w1
    b0, b1 = jnp.exp(-(degree + 1.0) * log0) * w0, jnp.exp(-(degree + 1.0) * log1) * w1
    factor = FOUR_PI / (2.0 * degree + 1.0)

    mine = pl.ds(pl.multiple_of(core * base, LANES), window)

    def align(value):
        return pltpu.roll(value, lax.rem(window - core * shift, window), 1)[:, :wide]

    def make_density(slot):
        for k in range(2):
            real = occ[slot, k * half : k * half + io]
            imag = occ[slot, k * half + io : (k + 1) * half]
            c_real, c_imag = cont[2 * k : 2 * k + 1], cont[2 * k + 1 : 2 * k + 2]
            top = slot * rows + k * half
            dens[top : top + io] = (real * c_real + imag * c_imag).astype(BF16)
            dens[top + io : top + half] = (real * c_imag - imag * c_real).astype(BF16)

    cont[...] = align(cont_ref[:, mine])
    occ[0] = align(occ_ref[:, mine].astype(F32))
    make_density(0)
    m_send[chunks - 1] = jnp.zeros(m_send.shape[1:], F32)
    m_own[chunks - 1] = jnp.zeros(m_own.shape[1:], F32)

    send_occ.wait()
    occ[1] = align(occ_in[...].astype(F32))
    make_density(1)
    fetch.wait()

    def m_copy(c):
        return pltpu.make_async_remote_copy(
            src_ref=m_send.at[c],
            dst_ref=m_recv.at[c],
            send_sem=m_send_sem.at[c],
            recv_sem=m_recv_sem.at[c],
            device_id={"orb": sibling},
            device_id_type=MESH,
        )

    def project(c):
        count = min(CHUNK, modes - c * CHUNK)
        part = lax.dot_general(
            dens[:, :points],
            table[c * CHUNK : c * CHUNK + count, :],
            (((1,), (1,)), ((), ())),
            preferred_element_type=F32,
        )
        m_own[c, :, :count] = part[:rows]
        m_send[c, :, :count] = part[rows:]
        m_copy(c).start()

    def up_copy(u):
        return pltpu.make_async_remote_copy(
            src_ref=st.at[u],
            dst_ref=inbox.at[me],
            send_sem=up_send.at[u],
            recv_sem=up_recv.at[me],
            device_id={"rad": u * stride},
            device_id_type=MESH,
        )

    def summarise(c):
        m_copy(c).wait()
        total = m_own[c] + m_recv[c]
        m_own[c] = total
        for u in range(c * CHUNK // LANES, (c + 1) * CHUNK // LANES):
            cols = slice(u * LANES, (u + 1) * LANES)
            here = (u * LANES) % CHUNK
            m0 = total[:half, here : here + LANES]
            m1 = total[half:, here : here + LANES]
            st[u, :half] = (a0[:, cols] * m0 + a1[:, cols] * m1).astype(BF16)
            st[u, half:] = (b0[:, cols] * m0 + b1[:, cols] * m1).astype(BF16)

            @pl.when(me != u * stride)
            def _():
                up_copy(u).start()

    project(0)
    for c in range(1, chunks):
        project(c)
        summarise(c - 1)
    summarise(chunks - 1)

    my_unit = me // stride

    def back_copy(r):
        return pltpu.make_async_remote_copy(
            src_ref=carried.at[r],
            dst_ref=carry.at[my_unit],
            send_sem=back_send.at[r],
            recv_sem=back_recv.at[my_unit],
            device_id={"rad": r},
            device_id_type=MESH,
        )

    def own_unit():
        inbox[me] = st[my_unit]

        def receive(r, held):
            @pl.when(r != me)
            def _():
                pltpu.make_async_remote_copy(
                    src_ref=st.at[0],
                    dst_ref=inbox.at[r],
                    send_sem=up_send.at[0],
                    recv_sem=up_recv.at[r],
                    device_id={"rad": r},
                    device_id_type=MESH,
                ).wait_recv()
            return held

        def rising(r, total):
            carried[r, :half] = total.astype(BF16)
            return total + inbox[r, :half].astype(F32)

        def falling(step, total):
            r = n_rad - 1 - step
            carried[r, half:] = total.astype(BF16)

            @pl.when(r != me)
            def _():
                back_copy(r).start()

            return total + inbox[r, half:].astype(F32)

        zero = jnp.zeros((half, LANES), F32)
        lax.fori_loop(0, n_rad, receive, 0)
        lax.fori_loop(0, n_rad, rising, zero, unroll=n_rad <= 8)
        lax.fori_loop(0, n_rad, falling, zero, unroll=n_rad <= 8)
        carry[my_unit] = carried[me]

    if stride == 1:
        own_unit()
    else:
        pl.when(lax.rem(me, stride) == 0)(own_unit)

    for u in range(units):
        @pl.when(me != u * stride)
        def _():
            pltpu.make_async_remote_copy(
                src_ref=carried.at[0],
                dst_ref=carry.at[u],
                send_sem=back_send.at[0],
                recv_sem=back_recv.at[u],
                device_id={"rad": u * stride},
                device_id_type=MESH,
            ).wait_recv()

        cols = slice(u * LANES, (u + 1) * LANES)
        here = (u * LANES) % CHUNK
        total = m_own[u * LANES // CHUNK]
        m0 = total[:half, here : here + LANES]
        m1 = total[half:, here : here + LANES]
        inner = carry[u, :half].astype(F32)
        outer = carry[u, half:].astype(F32)
        inner0 = w0 * m0 + down0[:, cols] * inner
        outer0 = up0[:, cols] * (b1[:, cols] * m1 + outer)
        inner1 = w1 * m1 + down1[:, cols] * (a0[:, cols] * m0 + inner)
        outer1 = up1[:, cols] * outer
        pot[:half, cols] = (factor[:, cols] * (inner0 / r0 + outer0)).astype(BF16)
        pot[half:rows, cols] = (factor[:, cols] * (inner1 / r1 + outer1)).astype(BF16)

    send_pot = pltpu.make_async_remote_copy(
        src_ref=pot.at[0:rows],
        dst_ref=pot.at[rows : 2 * rows],
        send_sem=sib_send.at[1],
        recv_sem=sib_recv.at[1],
        device_id={"orb": sibling},
        device_id_type=MESH,
    )
    send_pot.start()
    send_pot.wait()

    potential = pot[:, :modes]
    for start in range(0, points, CHUNK):
        count = min(CHUNK, points - start)
        span = slice(start, start + count)
        grid = jnp.dot(potential, table[:, span], preferred_element_type=F32)
        for k in range(2):
            real_sum = imag_sum = None
            for slot in range(2):
                top = k * half
                o_real = occ[slot, top : top + io, span]
                o_imag = occ[slot, top + io : top + half, span]
                top += slot * rows
                g_real, g_imag = grid[top : top + io], grid[top + io : top + half]
                real = o_real * g_real - o_imag * g_imag
                imag = o_real * g_imag + o_imag * g_real
                real_sum = real if slot == 0 else real_sum + real
                imag_sum = imag if slot == 0 else imag_sum + imag
            out_ref[k : k + 1, span] = jnp.sum(real_sum, axis=0, keepdims=True)
            out_ref[2 + k : 3 + k, span] = jnp.sum(imag_sum, axis=0, keepdims=True)

    for u in range(units):
        @pl.when(me != u * stride)
        def _():
            up_copy(u).wait_send()

    def finish():
        def sent(r, held):
            @pl.when(r != me)
            def _():
                back_copy(r).wait_send()
            return held

        lax.fori_loop(0, n_rad, sent, 0)

    if stride == 1:
        finish()
    else:
        pl.when(lax.rem(me, stride) == 0)(finish)


def on_device(occupied, continuum, harmonics, angle_weight, radial_weight, radius, harmonic_order):
    io, _, radial, total_points = occupied.shape
    points, modes = harmonics.shape
    n_rad = lax.axis_size("rad")
    padded = -(-modes // CHUNK) * CHUNK
    units, chunks = padded // LANES, padded // CHUNK
    base = points // LANES * LANES
    wide = -(-points // LANES) * LANES
    window = -(-total_points // LANES) * LANES - base
    lanes_in = base + window
    rows = 4 * io
    half = 2 * io

    fill = ((0, 0), (0, lanes_in - total_points))
    occ_rows = jnp.pad(jnp.transpose(occupied, (2, 1, 0, 3)).reshape(rows, total_points), fill)
    weighted = continuum.astype(F32) * angle_weight
    cont_rows = jnp.pad(jnp.transpose(weighted, (1, 0, 2)).reshape(4, total_points), fill)
    degree = jnp.pad(degree_of(harmonic_order).astype(F32), (0, padded - modes))[None]

    vmem = pl.BlockSpec(memory_space=pltpu.VMEM)
    smem = pl.BlockSpec(memory_space=pltpu.SMEM)
    dma = pltpu.SemaphoreType.DMA
    field = pl.pallas_call(
        functools.partial(kernel, n_rad, io, points, modes),
        out_shape=jax.ShapeDtypeStruct((4, points), F32),
        in_specs=[vmem, vmem, vmem, smem, smem, pl.BlockSpec(memory_space=pl.ANY)],
        out_specs=vmem,
        scratch_shapes=[
            pltpu.VMEM((modes, points), BF16),
            pltpu.VMEM((rows, window), BF16),
            pltpu.VMEM((2, rows, wide), F32),
            pltpu.VMEM((4, wide), F32),
            pltpu.VMEM((2 * rows, wide), BF16),
            pltpu.VMEM((chunks, rows, CHUNK), F32),
            pltpu.VMEM((chunks, rows, CHUNK), F32),
            pltpu.VMEM((chunks, rows, CHUNK), F32),
            pltpu.VMEM((units, 2 * half, LANES), BF16),
            pltpu.VMEM((n_rad, 2 * half, LANES), BF16),
            pltpu.VMEM((n_rad, 2 * half, LANES), BF16),
            pltpu.VMEM((units, 2 * half, LANES), BF16),
            pltpu.VMEM((2 * rows, padded), BF16),
            dma,
            dma((2,)),
            dma((2,)),
            dma((chunks,)),
            dma((chunks,)),
            dma((units,)),
            dma((n_rad,)),
            dma((n_rad,)),
            dma((units,)),
        ],
        compiler_params=pltpu.CompilerParams(
            collective_id=0, has_side_effects=True, vmem_limit_bytes=48 * 1024 * 1024
        ),
        cost_estimate=pl.CostEstimate(
            flops=8 * rows * points * modes, bytes_accessed=2 * points * modes, transcendentals=0
        ),
    )(occ_rows, cont_rows, degree, radius, radial_weight, harmonics.T)
    return field.reshape(2, radial, points)


def solution(mesh):
    placed = (
        P("orb", None, "rad", None),
        P(None, ("grp", "rad"), None),
        P("orb", None),
        P(),
        P("rad"),
        P("rad"),
        P(),
    )
    return jax.shard_map(
        on_device,
        mesh=mesh,
        in_specs=placed,
        out_specs=P(None, ("grp", "rad"), "orb"),
        check_vma=False,
    )
```

```python
import functools

import jax
import jax.numpy as jnp
from jax import lax
from jax.experimental import pallas as pl
from jax.experimental.pallas import tpu as pltpu
from jax.sharding import PartitionSpec as P

LMAX = 30
FOUR_PI = 12.566370614359172
MESH = pl.DeviceIdType.MESH
LANES = 128
CHUNK = 256
F32 = jnp.float32
BF16 = jnp.bfloat16


def degree_of(harmonic_order):
    degree = jnp.zeros(harmonic_order.shape, F32)
    for least in range(1, LMAX + 1):
        degree += (harmonic_order >= least * least).astype(F32)
    return degree


def kernel(
    n_rad, io, points, modes,
    occ_hbm, cont_hbm, angle_hbm, order_hbm, radius_hbm, weight_hbm, table_hbm, out_ref,
    cont_in, angle, order, padded_order, radius_ref, weight_ref, small_sem,
    table, occ_raw, occ, cont, dens, m_own, m_send, m_recv, st, inbox, carried, carry, pot,
    table_sem, sib_send, sib_recv, m_send_sem, m_recv_sem, up_send, up_recv, back_send, back_recv,
):
    me, core = lax.axis_index("rad"), lax.axis_index("orb")
    sibling = 1 - core
    rows = 4 * io
    half = 2 * io
    units = st.shape[0]
    stride = n_rad // units
    wide = occ.shape[2]
    base = points // LANES * LANES
    shift = points - base
    total_points = occ_raw.shape[-1]
    chunks = m_own.shape[0]

    small = [
        pltpu.make_async_copy(source, target, small_sem.at[place])
        for place, (source, target) in enumerate((
            (order_hbm, order), (radius_hbm, radius_ref), (weight_hbm, weight_ref),
            (cont_hbm, cont_in), (angle_hbm, angle), (occ_hbm, occ_raw.at[0]),
        ))
    ]
    for copy in small:
        copy.start()
    fetch = pltpu.make_async_copy(table_hbm, table, table_sem)
    fetch.start()

    barrier = pltpu.get_barrier_semaphore()
    pl.semaphore_signal(barrier, inc=1, device_id={"orb": sibling}, device_id_type=MESH)

    def greet(step, carry_in):
        other = lax.rem(me + step, n_rad)
        pl.semaphore_signal(barrier, inc=1, device_id={"rad": other}, device_id_type=MESH)
        return carry_in

    lax.fori_loop(1, n_rad, greet, 0)
    pl.semaphore_wait(barrier, n_rad)

    send_occ = pltpu.make_async_remote_copy(
        src_ref=occ_hbm,
        dst_ref=occ_raw.at[1],
        send_sem=sib_send.at[0],
        recv_sem=sib_recv.at[0],
        device_id={"orb": sibling},
        device_id_type=MESH,
    )
    send_occ.start()

    for copy in small:
        copy.wait()
    padded_order[...] = jnp.zeros(padded_order.shape, jnp.int32)
    padded_order[:, :modes] = order[...]
    degree = degree_of(padded_order[...])
    r0, r1, w0, w1 = radius_ref[0], radius_ref[1], weight_ref[0], weight_ref[1]
    log0 = jnp.log(jnp.full(degree.shape, r0, F32))
    log1 = jnp.log(jnp.full(degree.shape, r1, F32))
    up0, up1 = jnp.exp(degree * log0), jnp.exp(degree * log1)
    down0, down1 = jnp.exp(-degree * log0), jnp.exp(-degree * log1)
    a0, a1 = up0 * w0, up1 * w1
    b0, b1 = jnp.exp(-(degree + 1.0) * log0) * w0, jnp.exp(-(degree + 1.0) * log1) * w1
    factor = FOUR_PI / (2.0 * degree + 1.0)

    def align(value):
        high = jnp.pad(value[:, base:], ((0, 0), (0, base + wide - total_points + LANES)))
        moved = pltpu.roll(high, high.shape[1] - shift, 1)[:, :wide]
        return jnp.where(core == 0, value[:, :wide], moved)

    def load_orbitals(slot):
        for c in range(2):
            both = occ_raw[slot, :, c].astype(F32)
            for k in range(2):
                top = k * half + c * io
                occ[slot, top : top + io] = align(both[:, k])

    def make_density(slot):
        for k in range(2):
            real = occ[slot, k * half : k * half + io]
            imag = occ[slot, k * half + io : (k + 1) * half]
            c_real, c_imag = cont[2 * k : 2 * k + 1], cont[2 * k + 1 : 2 * k + 2]
            top = slot * rows + k * half
            dens[top : top + io] = (real * c_real + imag * c_imag).astype(BF16)
            dens[top + io : top + half] = (real * c_imag - imag * c_real).astype(BF16)

    for c in range(2):
        wave = align(cont_in[c].astype(F32) * angle[...].reshape(1, total_points))
        for k in range(2):
            cont[2 * k + c : 2 * k + c + 1] = wave[k : k + 1]
    load_orbitals(0)
    make_density(0)
    m_send[chunks - 1] = jnp.zeros(m_send.shape[1:], F32)
    m_own[chunks - 1] = jnp.zeros(m_own.shape[1:], F32)

    send_occ.wait()
    load_orbitals(1)
    make_density(1)
    fetch.wait()

    def m_copy(c):
        return pltpu.make_async_remote_copy(
            src_ref=m_send.at[c],
            dst_ref=m_recv.at[c],
            send_sem=m_send_sem.at[c],
            recv_sem=m_recv_sem.at[c],
            device_id={"orb": sibling},
            device_id_type=MESH,
        )

    def project(c):
        count = min(CHUNK, modes - c * CHUNK)
        part = lax.dot_general(
            dens[:, :points],
            table[c * CHUNK : c * CHUNK + count, :],
            (((1,), (1,)), ((), ())),
            preferred_element_type=F32,
        )
        m_own[c, :, :count] = part[:rows]
        m_send[c, :, :count] = part[rows:]
        m_copy(c).start()

    def up_copy(u):
        return pltpu.make_async_remote_copy(
            src_ref=st.at[u],
            dst_ref=inbox.at[me],
            send_sem=up_send.at[u],
            recv_sem=up_recv.at[me],
            device_id={"rad": u * stride},
            device_id_type=MESH,
        )

    def summarise(c):
        m_copy(c).wait()
        total = m_own[c] + m_recv[c]
        m_own[c] = total
        for u in range(c * CHUNK // LANES, (c + 1) * CHUNK // LANES):
            cols = slice(u * LANES, (u + 1) * LANES)
            here = (u * LANES) % CHUNK
            m0 = total[:half, here : here + LANES]
            m1 = total[half:, here : here + LANES]
            st[u, :half] = (a0[:, cols] * m0 + a1[:, cols] * m1).astype(BF16)
            st[u, half:] = (b0[:, cols] * m0 + b1[:, cols] * m1).astype(BF16)

            @pl.when(me != u * stride)
            def _():
                up_copy(u).start()

    project(0)
    for c in range(1, chunks):
        project(c)
        summarise(c - 1)
    summarise(chunks - 1)

    my_unit = me // stride

    def back_copy(r):
        return pltpu.make_async_remote_copy(
            src_ref=carried.at[r],
            dst_ref=carry.at[my_unit],
            send_sem=back_send.at[r],
            recv_sem=back_recv.at[my_unit],
            device_id={"rad": r},
            device_id_type=MESH,
        )

    def own_unit():
        inbox[me] = st[my_unit]

        def receive(r, held):
            @pl.when(r != me)
            def _():
                pltpu.make_async_remote_copy(
                    src_ref=st.at[0],
                    dst_ref=inbox.at[r],
                    send_sem=up_send.at[0],
                    recv_sem=up_recv.at[r],
                    device_id={"rad": r},
                    device_id_type=MESH,
                ).wait_recv()
            return held

        def rising(r, total):
            carried[r, :half] = total.astype(BF16)
            return total + inbox[r, :half].astype(F32)

        def falling(step, total):
            r = n_rad - 1 - step
            carried[r, half:] = total.astype(BF16)

            @pl.when(r != me)
            def _():
                back_copy(r).start()

            return total + inbox[r, half:].astype(F32)

        zero = jnp.zeros((half, LANES), F32)
        lax.fori_loop(0, n_rad, receive, 0)
        lax.fori_loop(0, n_rad, rising, zero, unroll=n_rad <= 8)
        lax.fori_loop(0, n_rad, falling, zero, unroll=n_rad <= 8)
        carry[my_unit] = carried[me]

    if stride == 1:
        own_unit()
    else:
        pl.when(lax.rem(me, stride) == 0)(own_unit)

    for u in range(units):
        @pl.when(me != u * stride)
        def _():
            pltpu.make_async_remote_copy(
                src_ref=carried.at[0],
                dst_ref=carry.at[u],
                send_sem=back_send.at[0],
                recv_sem=back_recv.at[u],
                device_id={"rad": u * stride},
                device_id_type=MESH,
            ).wait_recv()

        cols = slice(u * LANES, (u + 1) * LANES)
        here = (u * LANES) % CHUNK
        total = m_own[u * LANES // CHUNK]
        m0 = total[:half, here : here + LANES]
        m1 = total[half:, here : here + LANES]
        inner = carry[u, :half].astype(F32)
        outer = carry[u, half:].astype(F32)
        inner0 = w0 * m0 + down0[:, cols] * inner
        outer0 = up0[:, cols] * (b1[:, cols] * m1 + outer)
        inner1 = w1 * m1 + down1[:, cols] * (a0[:, cols] * m0 + inner)
        outer1 = up1[:, cols] * outer
        pot[:half, cols] = (factor[:, cols] * (inner0 / r0 + outer0)).astype(BF16)
        pot[half:rows, cols] = (factor[:, cols] * (inner1 / r1 + outer1)).astype(BF16)

    send_pot = pltpu.make_async_remote_copy(
        src_ref=pot.at[0:rows],
        dst_ref=pot.at[rows : 2 * rows],
        send_sem=sib_send.at[1],
        recv_sem=sib_recv.at[1],
        device_id={"orb": sibling},
        device_id_type=MESH,
    )
    send_pot.start()
    send_pot.wait()

    potential = pot[:, :modes]
    for start in range(0, points, CHUNK):
        count = min(CHUNK, points - start)
        span = slice(start, start + count)
        grid = jnp.dot(potential, table[:, span], preferred_element_type=F32)
        for k in range(2):
            real_sum = imag_sum = None
            for slot in range(2):
                top = k * half
                o_real = occ[slot, top : top + io, span]
                o_imag = occ[slot, top + io : top + half, span]
                top += slot * rows
                g_real, g_imag = grid[top : top + io], grid[top + io : top + half]
                real = o_real * g_real - o_imag * g_imag
                imag = o_real * g_imag + o_imag * g_real
                real_sum = real if slot == 0 else real_sum + real
                imag_sum = imag if slot == 0 else imag_sum + imag
            out_ref[k : k + 1, span] = jnp.sum(real_sum, axis=0, keepdims=True)
            out_ref[2 + k : 3 + k, span] = jnp.sum(imag_sum, axis=0, keepdims=True)

    for u in range(units):
        @pl.when(me != u * stride)
        def _():
            up_copy(u).wait_send()

    def finish():
        def sent(r, held):
            @pl.when(r != me)
            def _():
                back_copy(r).wait_send()
            return held

        lax.fori_loop(0, n_rad, sent, 0)

    if stride == 1:
        finish()
    else:
        pl.when(lax.rem(me, stride) == 0)(finish)


def on_device(occupied, continuum, harmonics, angle_weight, radial_weight, radius, harmonic_order):
    io, _, radial, total_points = occupied.shape
    points, modes = harmonics.shape
    n_rad = lax.axis_size("rad")
    padded = -(-modes // CHUNK) * CHUNK
    units, chunks = padded // LANES, padded // CHUNK
    wide = -(-points // LANES) * LANES
    rows = 4 * io
    half = 2 * io

    vmem = pl.BlockSpec(memory_space=pltpu.VMEM)
    dma = pltpu.SemaphoreType.DMA
    field = pl.pallas_call(
        functools.partial(kernel, n_rad, io, points, modes),
        out_shape=jax.ShapeDtypeStruct((4, points), F32),
        in_specs=[pl.BlockSpec(memory_space=pl.ANY)] * 7,
        out_specs=vmem,
        scratch_shapes=[
            pltpu.VMEM(continuum.shape, BF16),
            pltpu.VMEM(angle_weight.shape, F32),
            pltpu.VMEM((1, modes), jnp.int32),
            pltpu.VMEM((1, padded), jnp.int32),
            pltpu.SMEM(radius.shape, F32),
            pltpu.SMEM(radius.shape, F32),
            dma((6,)),
            pltpu.VMEM((modes, points), BF16),
            pltpu.VMEM((2, *occupied.shape), BF16),
            pltpu.VMEM((2, rows, wide), F32),
            pltpu.VMEM((4, wide), F32),
            pltpu.VMEM((2 * rows, wide), BF16),
            pltpu.VMEM((chunks, rows, CHUNK), F32),
            pltpu.VMEM((chunks, rows, CHUNK), F32),
            pltpu.VMEM((chunks, rows, CHUNK), F32),
            pltpu.VMEM((units, 2 * half, LANES), BF16),
            pltpu.VMEM((n_rad, 2 * half, LANES), BF16),
            pltpu.VMEM((n_rad, 2 * half, LANES), BF16),
            pltpu.VMEM((units, 2 * half, LANES), BF16),
            pltpu.VMEM((2 * rows, padded), BF16),
            dma,
            dma((2,)),
            dma((2,)),
            dma((chunks,)),
            dma((chunks,)),
            dma((units,)),
            dma((n_rad,)),
            dma((n_rad,)),
            dma((units,)),
        ],
        compiler_params=pltpu.CompilerParams(
            collective_id=0, has_side_effects=True, vmem_limit_bytes=63 * 1024 * 1024
        ),
        cost_estimate=pl.CostEstimate(
            flops=8 * rows * points * modes, bytes_accessed=2 * points * modes, transcendentals=0
        ),
    )(
        occupied, continuum, angle_weight, harmonic_order[None], radius, radial_weight,
        harmonics.T,
    )
    return field.reshape(2, radial, points)


def solution(mesh):
    placed = (
        P("orb", None, "rad", None),
        P(None, ("grp", "rad"), None),
        P("orb", None),
        P(),
        P("rad"),
        P("rad"),
        P(),
    )
    return jax.shard_map(
        on_device,
        mesh=mesh,
        in_specs=placed,
        out_specs=P(None, ("grp", "rad"), "orb"),
        check_vma=False,
    )
```

```python
import functools

import jax
import jax.numpy as jnp
from jax import lax
from jax.experimental import pallas as pl
from jax.experimental.pallas import tpu as pltpu
from jax.sharding import PartitionSpec as P

LMAX = 30
FOUR_PI = 12.566370614359172
MESH = pl.DeviceIdType.MESH
LANES = 128
CHUNK = 256
F32 = jnp.float32
BF16 = jnp.bfloat16


def degree_of(harmonic_order):
    degree = jnp.zeros(harmonic_order.shape, F32)
    for least in range(1, LMAX + 1):
        degree += (harmonic_order >= least * least).astype(F32)
    return degree


def kernel(
    n_rad, io, points, modes,
    occ_hbm, cont_hbm, angle_hbm, order_hbm, radius_hbm, weight_hbm, table_hbm, out_ref,
    cont_in, angle, order, padded_order, radius_ref, weight_ref, small_sem,
    table, occ_raw, occ, cont, dens, m_own, m_send, m_recv, st, inbox, carried, carry, pot,
    table_sem, sib_send, sib_recv, m_send_sem, m_recv_sem, up_send, up_recv, back_send, back_recv,
):
    me, core = lax.axis_index("rad"), lax.axis_index("orb")
    sibling = 1 - core
    rows = 4 * io
    half = 2 * io
    units = st.shape[0]
    stride = n_rad // units
    outer_slots = [slot for slot in range(units) if not units // 4 <= slot < 3 * units // 4]
    inner_slots = [slot for slot in range(units) if units // 4 <= slot < 3 * units // 4]
    owners = [slot * stride for slot in outer_slots + inner_slots]
    wide = occ.shape[2]
    base = points // LANES * LANES
    shift = points - base
    total_points = occ_raw.shape[-1]
    chunks = m_own.shape[0]

    small = [
        pltpu.make_async_copy(source, target, small_sem.at[place])
        for place, (source, target) in enumerate((
            (order_hbm, order), (radius_hbm, radius_ref), (weight_hbm, weight_ref),
            (cont_hbm, cont_in), (angle_hbm, angle), (occ_hbm, occ_raw.at[0]),
        ))
    ]
    for copy in small:
        copy.start()
    fetch = pltpu.make_async_copy(table_hbm, table, table_sem)
    fetch.start()

    barrier = pltpu.get_barrier_semaphore()
    pl.semaphore_signal(barrier, inc=1, device_id={"orb": sibling}, device_id_type=MESH)

    def greet(step, carry_in):
        other = lax.rem(me + step, n_rad)
        pl.semaphore_signal(barrier, inc=1, device_id={"rad": other}, device_id_type=MESH)
        return carry_in

    lax.fori_loop(1, n_rad, greet, 0)
    pl.semaphore_wait(barrier, n_rad)

    send_occ = pltpu.make_async_remote_copy(
        src_ref=occ_hbm,
        dst_ref=occ_raw.at[1],
        send_sem=sib_send.at[0],
        recv_sem=sib_recv.at[0],
        device_id={"orb": sibling},
        device_id_type=MESH,
    )
    send_occ.start()

    for copy in small:
        copy.wait()
    padded_order[...] = jnp.zeros(padded_order.shape, jnp.int32)
    padded_order[:, :modes] = order[...]
    degree = degree_of(padded_order[...])
    r0, r1, w0, w1 = radius_ref[0], radius_ref[1], weight_ref[0], weight_ref[1]
    log0 = jnp.log(jnp.full(degree.shape, r0, F32))
    log1 = jnp.log(jnp.full(degree.shape, r1, F32))
    up0, up1 = jnp.exp(degree * log0), jnp.exp(degree * log1)
    down0, down1 = jnp.exp(-degree * log0), jnp.exp(-degree * log1)
    a0, a1 = up0 * w0, up1 * w1
    b0, b1 = jnp.exp(-(degree + 1.0) * log0) * w0, jnp.exp(-(degree + 1.0) * log1) * w1
    factor = FOUR_PI / (2.0 * degree + 1.0)

    def align(value):
        high = jnp.pad(value[:, base:], ((0, 0), (0, base + wide - total_points + LANES)))
        moved = pltpu.roll(high, high.shape[1] - shift, 1)[:, :wide]
        return jnp.where(core == 0, value[:, :wide], moved)

    def load_orbitals(slot):
        for c in range(2):
            both = occ_raw[slot, :, c].astype(F32)
            for k in range(2):
                top = k * half + c * io
                occ[slot, top : top + io] = align(both[:, k])

    def make_density(slot):
        for k in range(2):
            real = occ[slot, k * half : k * half + io]
            imag = occ[slot, k * half + io : (k + 1) * half]
            c_real, c_imag = cont[2 * k : 2 * k + 1], cont[2 * k + 1 : 2 * k + 2]
            top = slot * rows + k * half
            dens[top : top + io] = (real * c_real + imag * c_imag).astype(BF16)
            dens[top + io : top + half] = (real * c_imag - imag * c_real).astype(BF16)

    for c in range(2):
        wave = align(cont_in[c].astype(F32) * angle[...].reshape(1, total_points))
        for k in range(2):
            cont[2 * k + c : 2 * k + c + 1] = wave[k : k + 1]
    load_orbitals(0)
    make_density(0)
    m_send[chunks - 1] = jnp.zeros(m_send.shape[1:], F32)
    m_own[chunks - 1] = jnp.zeros(m_own.shape[1:], F32)

    send_occ.wait()
    load_orbitals(1)
    make_density(1)
    fetch.wait()

    def m_copy(c):
        return pltpu.make_async_remote_copy(
            src_ref=m_send.at[c],
            dst_ref=m_recv.at[c],
            send_sem=m_send_sem.at[c],
            recv_sem=m_recv_sem.at[c],
            device_id={"orb": sibling},
            device_id_type=MESH,
        )

    def project(c):
        count = min(CHUNK, modes - c * CHUNK)
        part = lax.dot_general(
            dens[:, :points],
            table[c * CHUNK : c * CHUNK + count, :],
            (((1,), (1,)), ((), ())),
            preferred_element_type=F32,
        )
        m_own[c, :, :count] = part[:rows]
        m_send[c, :, :count] = part[rows:]
        m_copy(c).start()

    def up_copy(u):
        return pltpu.make_async_remote_copy(
            src_ref=st.at[u],
            dst_ref=inbox.at[me],
            send_sem=up_send.at[u],
            recv_sem=up_recv.at[me],
            device_id={"rad": owners[u]},
            device_id_type=MESH,
        )

    def summarise(c):
        m_copy(c).wait()
        total = m_own[c] + m_recv[c]
        m_own[c] = total
        for u in range(c * CHUNK // LANES, (c + 1) * CHUNK // LANES):
            cols = slice(u * LANES, (u + 1) * LANES)
            here = (u * LANES) % CHUNK
            m0 = total[:half, here : here + LANES]
            m1 = total[half:, here : here + LANES]
            st[u, :half] = (a0[:, cols] * m0 + a1[:, cols] * m1).astype(BF16)
            st[u, half:] = (b0[:, cols] * m0 + b1[:, cols] * m1).astype(BF16)

            @pl.when(me != owners[u])
            def _():
                up_copy(u).start()

    def back_copy(u, r):
        return pltpu.make_async_remote_copy(
            src_ref=carried.at[r],
            dst_ref=carry.at[u],
            send_sem=back_send.at[r],
            recv_sem=back_recv.at[u],
            device_id={"rad": r},
            device_id_type=MESH,
        )

    def own_unit(u):
        inbox[owners[u]] = st[u]

        def receive(r, held):
            @pl.when(r != me)
            def _():
                pltpu.make_async_remote_copy(
                    src_ref=st.at[0],
                    dst_ref=inbox.at[r],
                    send_sem=up_send.at[0],
                    recv_sem=up_recv.at[r],
                    device_id={"rad": r},
                    device_id_type=MESH,
                ).wait_recv()
            return held

        def rising(r, total):
            carried[r, :half] = total.astype(BF16)
            return total + inbox[r, :half].astype(F32)

        def falling(step, total):
            r = n_rad - 1 - step
            carried[r, half:] = total.astype(BF16)

            @pl.when(r != me)
            def _():
                back_copy(u, r).start()

            return total + inbox[r, half:].astype(F32)

        zero = jnp.zeros((half, LANES), F32)
        lax.fori_loop(0, n_rad, receive, 0)
        lax.fori_loop(0, n_rad, rising, zero, unroll=n_rad <= 8)
        lax.fori_loop(0, n_rad, falling, zero, unroll=n_rad <= 8)
        carry[u] = carried[owners[u]]

    def serve(c):
        for u in range(c * CHUNK // LANES, (c + 1) * CHUNK // LANES):
            pl.when(me == owners[u])(functools.partial(own_unit, u))

    project(0)
    for c in range(1, chunks):
        project(c)
        summarise(c - 1)
    summarise(chunks - 1)
    for c in range(chunks):
        serve(c)

    for u in range(units):
        @pl.when(me != owners[u])
        def _():
            pltpu.make_async_remote_copy(
                src_ref=carried.at[0],
                dst_ref=carry.at[u],
                send_sem=back_send.at[0],
                recv_sem=back_recv.at[u],
                device_id={"rad": owners[u]},
                device_id_type=MESH,
            ).wait_recv()

        cols = slice(u * LANES, (u + 1) * LANES)
        here = (u * LANES) % CHUNK
        total = m_own[u * LANES // CHUNK]
        m0 = total[:half, here : here + LANES]
        m1 = total[half:, here : here + LANES]
        inner = carry[u, :half].astype(F32)
        outer = carry[u, half:].astype(F32)
        inner0 = w0 * m0 + down0[:, cols] * inner
        outer0 = up0[:, cols] * (b1[:, cols] * m1 + outer)
        inner1 = w1 * m1 + down1[:, cols] * (a0[:, cols] * m0 + inner)
        outer1 = up1[:, cols] * outer
        pot[:half, cols] = (factor[:, cols] * (inner0 / r0 + outer0)).astype(BF16)
        pot[half:rows, cols] = (factor[:, cols] * (inner1 / r1 + outer1)).astype(BF16)

    send_pot = pltpu.make_async_remote_copy(
        src_ref=pot.at[0:rows],
        dst_ref=pot.at[rows : 2 * rows],
        send_sem=sib_send.at[1],
        recv_sem=sib_recv.at[1],
        device_id={"orb": sibling},
        device_id_type=MESH,
    )
    send_pot.start()
    send_pot.wait()

    potential = pot[:, :modes]
    for start in range(0, points, CHUNK):
        count = min(CHUNK, points - start)
        span = slice(start, start + count)
        grid = jnp.dot(potential, table[:, span], preferred_element_type=F32)
        for k in range(2):
            real_sum = imag_sum = None
            for slot in range(2):
                top = k * half
                o_real = occ[slot, top : top + io, span]
                o_imag = occ[slot, top + io : top + half, span]
                top += slot * rows
                g_real, g_imag = grid[top : top + io], grid[top + io : top + half]
                real = o_real * g_real - o_imag * g_imag
                imag = o_real * g_imag + o_imag * g_real
                real_sum = real if slot == 0 else real_sum + real
                imag_sum = imag if slot == 0 else imag_sum + imag
            out_ref[0, k : k + 1, span] = jnp.sum(real_sum, axis=0, keepdims=True)
            out_ref[1, k : k + 1, span] = jnp.sum(imag_sum, axis=0, keepdims=True)

    for u in range(units):
        @pl.when(me != owners[u])
        def _():
            up_copy(u).wait_send()

    for u in range(units):
        @pl.when(me == owners[u])
        def _():
            def sent(r, held):
                @pl.when(r != me)
                def _():
                    back_copy(u, r).wait_send()
                return held

            lax.fori_loop(0, n_rad, sent, 0)


def on_device(occupied, continuum, harmonics, angle_weight, radial_weight, radius, harmonic_order):
    io, _, radial, total_points = occupied.shape
    points, modes = harmonics.shape
    n_rad = lax.axis_size("rad")
    padded = -(-modes // CHUNK) * CHUNK
    units, chunks = padded // LANES, padded // CHUNK
    wide = -(-points // LANES) * LANES
    rows = 4 * io
    half = 2 * io

    vmem = pl.BlockSpec(memory_space=pltpu.VMEM)
    dma = pltpu.SemaphoreType.DMA
    field = pl.pallas_call(
        functools.partial(kernel, n_rad, io, points, modes),
        out_shape=jax.ShapeDtypeStruct((2, radial, points), F32),
        in_specs=[pl.BlockSpec(memory_space=pl.ANY)] * 7,
        out_specs=vmem,
        scratch_shapes=[
            pltpu.VMEM(continuum.shape, BF16),
            pltpu.VMEM(angle_weight.shape, F32),
            pltpu.VMEM((1, modes), jnp.int32),
            pltpu.VMEM((1, padded), jnp.int32),
            pltpu.SMEM(radius.shape, F32),
            pltpu.SMEM(radius.shape, F32),
            dma((6,)),
            pltpu.VMEM((modes, points), BF16),
            pltpu.VMEM((2, *occupied.shape), BF16),
            pltpu.VMEM((2, rows, wide), F32),
            pltpu.VMEM((4, wide), F32),
            pltpu.VMEM((2 * rows, wide), BF16),
            pltpu.VMEM((chunks, rows, CHUNK), F32),
            pltpu.VMEM((chunks, rows, CHUNK), F32),
            pltpu.VMEM((chunks, rows, CHUNK), F32),
            pltpu.VMEM((units, 2 * half, LANES), BF16),
            pltpu.VMEM((n_rad, 2 * half, LANES), BF16),
            pltpu.VMEM((n_rad, 2 * half, LANES), BF16),
            pltpu.VMEM((units, 2 * half, LANES), BF16),
            pltpu.VMEM((2 * rows, padded), BF16),
            dma,
            dma((2,)),
            dma((2,)),
            dma((chunks,)),
            dma((chunks,)),
            dma((units,)),
            dma((n_rad,)),
            dma((n_rad,)),
            dma((units,)),
        ],
        compiler_params=pltpu.CompilerParams(
            collective_id=0, has_side_effects=True, vmem_limit_bytes=63 * 1024 * 1024
        ),
        cost_estimate=pl.CostEstimate(
            flops=8 * rows * points * modes, bytes_accessed=2 * points * modes, transcendentals=0
        ),
    )(
        occupied, continuum, angle_weight, harmonic_order[None], radius, radial_weight,
        harmonics.T,
    )
    return field


def solution(mesh):
    placed = (
        P("orb", None, "rad", None),
        P(None, ("grp", "rad"), None),
        P("orb", None),
        P(),
        P("rad"),
        P("rad"),
        P(),
    )
    return jax.shard_map(
        on_device,
        mesh=mesh,
        in_specs=placed,
        out_specs=P(None, ("grp", "rad"), "orb"),
        check_vma=False,
    )
```

```python
import functools

import jax
import jax.numpy as jnp
from jax import lax
from jax.experimental import pallas as pl
from jax.experimental.pallas import tpu as pltpu
from jax.sharding import PartitionSpec as P

LMAX = 30
FOUR_PI = 12.566370614359172
MESH = pl.DeviceIdType.MESH
LANES = 128
CHUNK = 256
F32 = jnp.float32
BF16 = jnp.bfloat16


def degree_of(harmonic_order):
    degree = jnp.zeros(harmonic_order.shape, F32)
    for least in range(1, LMAX + 1):
        degree += (harmonic_order >= least * least).astype(F32)
    return degree


def kernel(
    n_rad, io, points, modes,
    occ_hbm, cont_hbm, angle_hbm, order_hbm, radius_hbm, weight_hbm, table_hbm, out_ref,
    cont_in, angle, order, padded_order, radius_ref, weight_ref, small_sem,
    table, occ_raw, occ, cont, dens, m_own, m_send, m_recv, st, inbox, carried, carry, pot,
    table_sem, sib_send, sib_recv, m_send_sem, m_recv_sem, up_send, up_recv, back_send, back_recv,
):
    me, core = lax.axis_index("rad"), lax.axis_index("orb")
    sibling = 1 - core
    rows = 4 * io
    half = 2 * io
    units = st.shape[0]
    stride = n_rad // units
    owners = []
    for slot in range(units // 2):
        owners += [slot * stride, (units - 1 - slot) * stride]
    wide = occ.shape[2]
    base = points // LANES * LANES
    shift = points - base
    total_points = occ_raw.shape[-1]
    chunks = m_own.shape[0]

    small = [
        pltpu.make_async_copy(source, target, small_sem.at[place])
        for place, (source, target) in enumerate((
            (order_hbm, order), (radius_hbm, radius_ref), (weight_hbm, weight_ref),
            (cont_hbm, cont_in), (angle_hbm, angle), (occ_hbm, occ_raw.at[0]),
        ))
    ]
    for copy in small:
        copy.start()
    fetch = pltpu.make_async_copy(table_hbm, table, table_sem)
    fetch.start()

    barrier = pltpu.get_barrier_semaphore()
    pl.semaphore_signal(barrier, inc=1, device_id={"orb": sibling}, device_id_type=MESH)

    def greet(step, carry_in):
        other = lax.rem(me + step, n_rad)
        pl.semaphore_signal(barrier, inc=1, device_id={"rad": other}, device_id_type=MESH)
        return carry_in

    lax.fori_loop(1, n_rad, greet, 0)
    pl.semaphore_wait(barrier, n_rad)

    send_occ = pltpu.make_async_remote_copy(
        src_ref=occ_hbm,
        dst_ref=occ_raw.at[1],
        send_sem=sib_send.at[0],
        recv_sem=sib_recv.at[0],
        device_id={"orb": sibling},
        device_id_type=MESH,
    )
    send_occ.start()

    for copy in small:
        copy.wait()
    padded_order[...] = jnp.zeros(padded_order.shape, jnp.int32)
    padded_order[:, :modes] = order[...]
    degree = degree_of(padded_order[...])
    r0, r1, w0, w1 = radius_ref[0], radius_ref[1], weight_ref[0], weight_ref[1]
    log0 = jnp.log(jnp.full(degree.shape, r0, F32))
    log1 = jnp.log(jnp.full(degree.shape, r1, F32))
    up0, up1 = jnp.exp(degree * log0), jnp.exp(degree * log1)
    down0, down1 = jnp.exp(-degree * log0), jnp.exp(-degree * log1)
    a0, a1 = up0 * w0, up1 * w1
    b0, b1 = jnp.exp(-(degree + 1.0) * log0) * w0, jnp.exp(-(degree + 1.0) * log1) * w1
    factor = FOUR_PI / (2.0 * degree + 1.0)

    def align(value):
        high = jnp.pad(value[:, base:], ((0, 0), (0, base + wide - total_points + LANES)))
        moved = pltpu.roll(high, high.shape[1] - shift, 1)[:, :wide]
        return jnp.where(core == 0, value[:, :wide], moved)

    def load_orbitals(slot):
        for c in range(2):
            both = occ_raw[slot, :, c].astype(F32)
            for k in range(2):
                top = k * half + c * io
                occ[slot, top : top + io] = align(both[:, k])

    def make_density(slot):
        for k in range(2):
            real = occ[slot, k * half : k * half + io]
            imag = occ[slot, k * half + io : (k + 1) * half]
            c_real, c_imag = cont[2 * k : 2 * k + 1], cont[2 * k + 1 : 2 * k + 2]
            top = slot * rows + k * half
            dens[top : top + io] = (real * c_real + imag * c_imag).astype(BF16)
            dens[top + io : top + half] = (real * c_imag - imag * c_real).astype(BF16)

    for c in range(2):
        wave = align(cont_in[c].astype(F32) * angle[...].reshape(1, total_points))
        for k in range(2):
            cont[2 * k + c : 2 * k + c + 1] = wave[k : k + 1]
    load_orbitals(0)
    make_density(0)
    m_send[chunks - 1] = jnp.zeros(m_send.shape[1:], F32)
    m_own[chunks - 1] = jnp.zeros(m_own.shape[1:], F32)

    send_occ.wait()
    load_orbitals(1)
    make_density(1)
    fetch.wait()

    def m_copy(c):
        return pltpu.make_async_remote_copy(
            src_ref=m_send.at[c],
            dst_ref=m_recv.at[c],
            send_sem=m_send_sem.at[c],
            recv_sem=m_recv_sem.at[c],
            device_id={"orb": sibling},
            device_id_type=MESH,
        )

    def project(c):
        count = min(CHUNK, modes - c * CHUNK)
        part = lax.dot_general(
            dens[:, :points],
            table[c * CHUNK : c * CHUNK + count, :],
            (((1,), (1,)), ((), ())),
            preferred_element_type=F32,
        )
        m_own[c, :, :count] = part[:rows]
        m_send[c, :, :count] = part[rows:]
        m_copy(c).start()

    def up_copy(u):
        return pltpu.make_async_remote_copy(
            src_ref=st.at[u],
            dst_ref=inbox.at[me],
            send_sem=up_send.at[u],
            recv_sem=up_recv.at[me],
            device_id={"rad": owners[u]},
            device_id_type=MESH,
        )

    def summarise(c):
        m_copy(c).wait()
        total = m_own[c] + m_recv[c]
        m_own[c] = total
        for u in range(c * CHUNK // LANES, (c + 1) * CHUNK // LANES):
            cols = slice(u * LANES, (u + 1) * LANES)
            here = (u * LANES) % CHUNK
            m0 = total[:half, here : here + LANES]
            m1 = total[half:, here : here + LANES]
            st[u, :half] = (a0[:, cols] * m0 + a1[:, cols] * m1).astype(BF16)
            st[u, half:] = (b0[:, cols] * m0 + b1[:, cols] * m1).astype(BF16)

            @pl.when(me != owners[u])
            def _():
                up_copy(u).start()

    def back_copy(u, r):
        return pltpu.make_async_remote_copy(
            src_ref=carried.at[r],
            dst_ref=carry.at[u],
            send_sem=back_send.at[r],
            recv_sem=back_recv.at[u],
            device_id={"rad": r},
            device_id_type=MESH,
        )

    def own_unit(u):
        inbox[owners[u]] = st[u]

        def receive(r, held):
            @pl.when(r != me)
            def _():
                pltpu.make_async_remote_copy(
                    src_ref=st.at[0],
                    dst_ref=inbox.at[r],
                    send_sem=up_send.at[0],
                    recv_sem=up_recv.at[r],
                    device_id={"rad": r},
                    device_id_type=MESH,
                ).wait_recv()
            return held

        def rising(r, total):
            carried[r, :half] = total.astype(BF16)
            return total + inbox[r, :half].astype(F32)

        def falling(step, total):
            r = n_rad - 1 - step
            carried[r, half:] = total.astype(BF16)

            @pl.when(r != me)
            def _():
                back_copy(u, r).start()

            return total + inbox[r, half:].astype(F32)

        zero = jnp.zeros((half, LANES), F32)
        lax.fori_loop(0, n_rad, receive, 0)
        lax.fori_loop(0, n_rad, rising, zero, unroll=n_rad <= 8)
        lax.fori_loop(0, n_rad, falling, zero, unroll=n_rad <= 8)
        carry[u] = carried[owners[u]]

    def serve(c):
        for u in range(c * CHUNK // LANES, (c + 1) * CHUNK // LANES):
            pl.when(me == owners[u])(functools.partial(own_unit, u))

    project(0)
    for c in range(1, chunks):
        project(c)
        summarise(c - 1)
    summarise(chunks - 1)
    for c in range(chunks):
        serve(c)

    for u in range(units):
        @pl.when(me != owners[u])
        def _():
            pltpu.make_async_remote_copy(
                src_ref=carried.at[0],
                dst_ref=carry.at[u],
                send_sem=back_send.at[0],
                recv_sem=back_recv.at[u],
                device_id={"rad": owners[u]},
                device_id_type=MESH,
            ).wait_recv()

        cols = slice(u * LANES, (u + 1) * LANES)
        here = (u * LANES) % CHUNK
        total = m_own[u * LANES // CHUNK]
        m0 = total[:half, here : here + LANES]
        m1 = total[half:, here : here + LANES]
        inner = carry[u, :half].astype(F32)
        outer = carry[u, half:].astype(F32)
        inner0 = w0 * m0 + down0[:, cols] * inner
        outer0 = up0[:, cols] * (b1[:, cols] * m1 + outer)
        inner1 = w1 * m1 + down1[:, cols] * (a0[:, cols] * m0 + inner)
        outer1 = up1[:, cols] * outer
        pot[:half, cols] = (factor[:, cols] * (inner0 / r0 + outer0)).astype(BF16)
        pot[half:rows, cols] = (factor[:, cols] * (inner1 / r1 + outer1)).astype(BF16)

    send_pot = pltpu.make_async_remote_copy(
        src_ref=pot.at[0:rows],
        dst_ref=pot.at[rows : 2 * rows],
        send_sem=sib_send.at[1],
        recv_sem=sib_recv.at[1],
        device_id={"orb": sibling},
        device_id_type=MESH,
    )
    send_pot.start()
    send_pot.wait()

    potential = pot[:, :modes]
    for start in range(0, points, CHUNK):
        count = min(CHUNK, points - start)
        span = slice(start, start + count)
        grid = jnp.dot(potential, table[:, span], preferred_element_type=F32)
        for k in range(2):
            real_sum = imag_sum = None
            for slot in range(2):
                top = k * half
                o_real = occ[slot, top : top + io, span]
                o_imag = occ[slot, top + io : top + half, span]
                top += slot * rows
                g_real, g_imag = grid[top : top + io], grid[top + io : top + half]
                real = o_real * g_real - o_imag * g_imag
                imag = o_real * g_imag + o_imag * g_real
                real_sum = real if slot == 0 else real_sum + real
                imag_sum = imag if slot == 0 else imag_sum + imag
            out_ref[0, k : k + 1, span] = jnp.sum(real_sum, axis=0, keepdims=True)
            out_ref[1, k : k + 1, span] = jnp.sum(imag_sum, axis=0, keepdims=True)

    for u in range(units):
        @pl.when(me != owners[u])
        def _():
            up_copy(u).wait_send()

    for u in range(units):
        @pl.when(me == owners[u])
        def _():
            def sent(r, held):
                @pl.when(r != me)
                def _():
                    back_copy(u, r).wait_send()
                return held

            lax.fori_loop(0, n_rad, sent, 0)


def on_device(occupied, continuum, harmonics, angle_weight, radial_weight, radius, harmonic_order):
    io, _, radial, total_points = occupied.shape
    points, modes = harmonics.shape
    n_rad = lax.axis_size("rad")
    padded = -(-modes // CHUNK) * CHUNK
    units, chunks = padded // LANES, padded // CHUNK
    wide = -(-points // LANES) * LANES
    rows = 4 * io
    half = 2 * io

    vmem = pl.BlockSpec(memory_space=pltpu.VMEM)
    dma = pltpu.SemaphoreType.DMA
    field = pl.pallas_call(
        functools.partial(kernel, n_rad, io, points, modes),
        out_shape=jax.ShapeDtypeStruct((2, radial, points), F32),
        in_specs=[pl.BlockSpec(memory_space=pl.ANY)] * 7,
        out_specs=vmem,
        scratch_shapes=[
            pltpu.VMEM(continuum.shape, BF16),
            pltpu.VMEM(angle_weight.shape, F32),
            pltpu.VMEM((1, modes), jnp.int32),
            pltpu.VMEM((1, padded), jnp.int32),
            pltpu.SMEM(radius.shape, F32),
            pltpu.SMEM(radius.shape, F32),
            dma((6,)),
            pltpu.VMEM((modes, points), BF16),
            pltpu.VMEM((2, *occupied.shape), BF16),
            pltpu.VMEM((2, rows, wide), F32),
            pltpu.VMEM((4, wide), F32),
            pltpu.VMEM((2 * rows, wide), BF16),
            pltpu.VMEM((chunks, rows, CHUNK), F32),
            pltpu.VMEM((chunks, rows, CHUNK), F32),
            pltpu.VMEM((chunks, rows, CHUNK), F32),
            pltpu.VMEM((units, 2 * half, LANES), BF16),
            pltpu.VMEM((n_rad, 2 * half, LANES), BF16),
            pltpu.VMEM((n_rad, 2 * half, LANES), BF16),
            pltpu.VMEM((units, 2 * half, LANES), BF16),
            pltpu.VMEM((2 * rows, padded), BF16),
            dma,
            dma((2,)),
            dma((2,)),
            dma((chunks,)),
            dma((chunks,)),
            dma((units,)),
            dma((n_rad,)),
            dma((n_rad,)),
            dma((units,)),
        ],
        compiler_params=pltpu.CompilerParams(
            collective_id=0, has_side_effects=True, vmem_limit_bytes=63 * 1024 * 1024
        ),
        cost_estimate=pl.CostEstimate(
            flops=8 * rows * points * modes, bytes_accessed=2 * points * modes, transcendentals=0
        ),
    )(
        occupied, continuum, angle_weight, harmonic_order[None], radius, radial_weight,
        harmonics.T,
    )
    return field


def solution(mesh):
    placed = (
        P("orb", None, "rad", None),
        P(None, ("grp", "rad"), None),
        P("orb", None),
        P(),
        P("rad"),
        P("rad"),
        P(),
    )
    return jax.shard_map(
        on_device,
        mesh=mesh,
        in_specs=placed,
        out_specs=P(None, ("grp", "rad"), "orb"),
        check_vma=False,
    )
```

```python
import functools

import jax
import jax.numpy as jnp
from jax import lax
from jax.experimental import pallas as pl
from jax.experimental.pallas import tpu as pltpu
from jax.sharding import PartitionSpec as P

LMAX = 30
FOUR_PI = 12.566370614359172
MESH = pl.DeviceIdType.MESH
LANES = 128
CHUNK = 512
F32 = jnp.float32
BF16 = jnp.bfloat16


def degree_of(harmonic_order):
    degree = jnp.zeros(harmonic_order.shape, F32)
    for least in range(1, LMAX + 1):
        degree += (harmonic_order >= least * least).astype(F32)
    return degree


def kernel(
    n_rad, io, points, modes,
    occ_hbm, cont_hbm, angle_hbm, order_hbm, radius_hbm, weight_hbm, table_hbm, out_ref,
    cont_in, angle, order, padded_order, radius_ref, weight_ref, small_sem,
    table, occ_raw, occ, cont, dens, m_own, m_send, m_recv, st, inbox, carried, carry, pot,
    table_sem, sib_send, sib_recv, m_send_sem, m_recv_sem, up_send, up_recv, back_send, back_recv,
):
    me, core = lax.axis_index("rad"), lax.axis_index("orb")
    sibling = 1 - core
    rows = 4 * io
    half = 2 * io
    units = st.shape[0]
    stride = n_rad // units
    owners = []
    for slot in range(units // 2):
        owners += [slot * stride, (units - 1 - slot) * stride]
    wide = occ.shape[2]
    base = points // LANES * LANES
    shift = points - base
    total_points = occ_raw.shape[-1]
    chunks = m_own.shape[0]

    small = [
        pltpu.make_async_copy(source, target, small_sem.at[place])
        for place, (source, target) in enumerate((
            (order_hbm, order), (radius_hbm, radius_ref), (weight_hbm, weight_ref),
            (cont_hbm, cont_in), (angle_hbm, angle), (occ_hbm, occ_raw.at[0]),
        ))
    ]
    for copy in small:
        copy.start()
    fetch = pltpu.make_async_copy(table_hbm, table, table_sem)
    fetch.start()

    barrier = pltpu.get_barrier_semaphore()
    pl.semaphore_signal(barrier, inc=1, device_id={"orb": sibling}, device_id_type=MESH)

    def greet(step, carry_in):
        other = lax.rem(me + step, n_rad)
        pl.semaphore_signal(barrier, inc=1, device_id={"rad": other}, device_id_type=MESH)
        return carry_in

    lax.fori_loop(1, n_rad, greet, 0)
    pl.semaphore_wait(barrier, n_rad)

    send_occ = pltpu.make_async_remote_copy(
        src_ref=occ_hbm,
        dst_ref=occ_raw.at[1],
        send_sem=sib_send.at[0],
        recv_sem=sib_recv.at[0],
        device_id={"orb": sibling},
        device_id_type=MESH,
    )
    send_occ.start()

    for copy in small:
        copy.wait()
    padded_order[...] = jnp.zeros(padded_order.shape, jnp.int32)
    padded_order[:, :modes] = order[...]
    degree = degree_of(padded_order[...])
    r0, r1, w0, w1 = radius_ref[0], radius_ref[1], weight_ref[0], weight_ref[1]
    log0 = jnp.log(jnp.full(degree.shape, r0, F32))
    log1 = jnp.log(jnp.full(degree.shape, r1, F32))
    up0, up1 = jnp.exp(degree * log0), jnp.exp(degree * log1)
    down0, down1 = jnp.exp(-degree * log0), jnp.exp(-degree * log1)
    a0, a1 = up0 * w0, up1 * w1
    b0, b1 = jnp.exp(-(degree + 1.0) * log0) * w0, jnp.exp(-(degree + 1.0) * log1) * w1
    factor = FOUR_PI / (2.0 * degree + 1.0)

    def align(value):
        high = jnp.pad(value[:, base:], ((0, 0), (0, base + wide - total_points + LANES)))
        moved = pltpu.roll(high, high.shape[1] - shift, 1)[:, :wide]
        return jnp.where(core == 0, value[:, :wide], moved)

    def load_orbitals(slot):
        for c in range(2):
            both = occ_raw[slot, :, c].astype(F32)
            for k in range(2):
                top = k * half + c * io
                occ[slot, top : top + io] = align(both[:, k])

    def make_density(slot):
        for k in range(2):
            real = occ[slot, k * half : k * half + io]
            imag = occ[slot, k * half + io : (k + 1) * half]
            c_real, c_imag = cont[2 * k : 2 * k + 1], cont[2 * k + 1 : 2 * k + 2]
            top = slot * rows + k * half
            dens[top : top + io] = (real * c_real + imag * c_imag).astype(BF16)
            dens[top + io : top + half] = (real * c_imag - imag * c_real).astype(BF16)

    for c in range(2):
        wave = align(cont_in[c].astype(F32) * angle[...].reshape(1, total_points))
        for k in range(2):
            cont[2 * k + c : 2 * k + c + 1] = wave[k : k + 1]
    load_orbitals(0)
    make_density(0)
    m_send[chunks - 1] = jnp.zeros(m_send.shape[1:], F32)
    m_own[chunks - 1] = jnp.zeros(m_own.shape[1:], F32)

    send_occ.wait()
    load_orbitals(1)
    make_density(1)
    fetch.wait()

    def m_copy(c):
        return pltpu.make_async_remote_copy(
            src_ref=m_send.at[c],
            dst_ref=m_recv.at[c],
            send_sem=m_send_sem.at[c],
            recv_sem=m_recv_sem.at[c],
            device_id={"orb": sibling},
            device_id_type=MESH,
        )

    def project(c):
        count = min(CHUNK, modes - c * CHUNK)
        part = lax.dot_general(
            dens[:, :points],
            table[c * CHUNK : c * CHUNK + count, :],
            (((1,), (1,)), ((), ())),
            preferred_element_type=F32,
        )
        m_own[c, :, :count] = part[:rows]
        m_send[c, :, :count] = part[rows:]
        m_copy(c).start()

    def up_copy(u):
        return pltpu.make_async_remote_copy(
            src_ref=st.at[u],
            dst_ref=inbox.at[me],
            send_sem=up_send.at[u],
            recv_sem=up_recv.at[me],
            device_id={"rad": owners[u]},
            device_id_type=MESH,
        )

    def summarise(c):
        m_copy(c).wait()
        total = m_own[c] + m_recv[c]
        m_own[c] = total
        for u in range(c * CHUNK // LANES, (c + 1) * CHUNK // LANES):
            cols = slice(u * LANES, (u + 1) * LANES)
            here = (u * LANES) % CHUNK
            m0 = total[:half, here : here + LANES]
            m1 = total[half:, here : here + LANES]
            st[u, :half] = (a0[:, cols] * m0 + a1[:, cols] * m1).astype(BF16)
            st[u, half:] = (b0[:, cols] * m0 + b1[:, cols] * m1).astype(BF16)

            @pl.when(me != owners[u])
            def _():
                up_copy(u).start()

    def back_copy(u, r):
        return pltpu.make_async_remote_copy(
            src_ref=carried.at[r],
            dst_ref=carry.at[u],
            send_sem=back_send.at[r],
            recv_sem=back_recv.at[u],
            device_id={"rad": r},
            device_id_type=MESH,
        )

    def own_unit(u):
        inbox[owners[u]] = st[u]

        def receive(r, held):
            @pl.when(r != me)
            def _():
                pltpu.make_async_remote_copy(
                    src_ref=st.at[0],
                    dst_ref=inbox.at[r],
                    send_sem=up_send.at[0],
                    recv_sem=up_recv.at[r],
                    device_id={"rad": r},
                    device_id_type=MESH,
                ).wait_recv()
            return held

        def rising(r, total):
            receive(r, 0)
            carried[r, :half] = total.astype(BF16)
            return total + inbox[r, :half].astype(F32)

        def falling(step, total):
            r = n_rad - 1 - step
            carried[r, half:] = total.astype(BF16)

            @pl.when(r != me)
            def _():
                back_copy(u, r).start()

            return total + inbox[r, half:].astype(F32)

        zero = jnp.zeros((half, LANES), F32)
        lax.fori_loop(0, n_rad, rising, zero, unroll=n_rad <= 8)
        lax.fori_loop(0, n_rad, falling, zero, unroll=n_rad <= 8)
        carry[u] = carried[owners[u]]

    def serve(c):
        for u in range(c * CHUNK // LANES, (c + 1) * CHUNK // LANES):
            pl.when(me == owners[u])(functools.partial(own_unit, u))

    project(0)
    for c in range(1, chunks):
        project(c)
        summarise(c - 1)
    summarise(chunks - 1)
    for c in range(chunks):
        serve(c)

    for u in range(units):
        @pl.when(me != owners[u])
        def _():
            pltpu.make_async_remote_copy(
                src_ref=carried.at[0],
                dst_ref=carry.at[u],
                send_sem=back_send.at[0],
                recv_sem=back_recv.at[u],
                device_id={"rad": owners[u]},
                device_id_type=MESH,
            ).wait_recv()

        cols = slice(u * LANES, (u + 1) * LANES)
        here = (u * LANES) % CHUNK
        total = m_own[u * LANES // CHUNK]
        m0 = total[:half, here : here + LANES]
        m1 = total[half:, here : here + LANES]
        inner = carry[u, :half].astype(F32)
        outer = carry[u, half:].astype(F32)
        inner0 = w0 * m0 + down0[:, cols] * inner
        outer0 = up0[:, cols] * (b1[:, cols] * m1 + outer)
        inner1 = w1 * m1 + down1[:, cols] * (a0[:, cols] * m0 + inner)
        outer1 = up1[:, cols] * outer
        pot[:half, cols] = (factor[:, cols] * (inner0 / r0 + outer0)).astype(BF16)
        pot[half:rows, cols] = (factor[:, cols] * (inner1 / r1 + outer1)).astype(BF16)

    send_pot = pltpu.make_async_remote_copy(
        src_ref=pot.at[0:rows],
        dst_ref=pot.at[rows : 2 * rows],
        send_sem=sib_send.at[1],
        recv_sem=sib_recv.at[1],
        device_id={"orb": sibling},
        device_id_type=MESH,
    )
    send_pot.start()
    send_pot.wait()

    potential = pot[:, :modes]
    for start in range(0, points, CHUNK):
        count = min(CHUNK, points - start)
        span = slice(start, start + count)
        grid = jnp.dot(potential, table[:, span], preferred_element_type=F32)
        for k in range(2):
            real_sum = imag_sum = None
            for slot in range(2):
                top = k * half
                o_real = occ[slot, top : top + io, span]
                o_imag = occ[slot, top + io : top + half, span]
                top += slot * rows
                g_real, g_imag = grid[top : top + io], grid[top + io : top + half]
                real = o_real * g_real - o_imag * g_imag
                imag = o_real * g_imag + o_imag * g_real
                real_sum = real if slot == 0 else real_sum + real
                imag_sum = imag if slot == 0 else imag_sum + imag
            out_ref[0, k : k + 1, span] = jnp.sum(real_sum, axis=0, keepdims=True)
            out_ref[1, k : k + 1, span] = jnp.sum(imag_sum, axis=0, keepdims=True)

    for u in range(units):
        @pl.when(me != owners[u])
        def _():
            up_copy(u).wait_send()

    for u in range(units):
        @pl.when(me == owners[u])
        def _():
            def sent(r, held):
                @pl.when(r != me)
                def _():
                    back_copy(u, r).wait_send()
                return held

            lax.fori_loop(0, n_rad, sent, 0)


def on_device(occupied, continuum, harmonics, angle_weight, radial_weight, radius, harmonic_order):
    io, _, radial, total_points = occupied.shape
    points, modes = harmonics.shape
    n_rad = lax.axis_size("rad")
    padded = -(-modes // CHUNK) * CHUNK
    units, chunks = padded // LANES, padded // CHUNK
    wide = -(-points // LANES) * LANES
    rows = 4 * io
    half = 2 * io

    vmem = pl.BlockSpec(memory_space=pltpu.VMEM)
    dma = pltpu.SemaphoreType.DMA
    field = pl.pallas_call(
        functools.partial(kernel, n_rad, io, points, modes),
        out_shape=jax.ShapeDtypeStruct((2, radial, points), F32),
        in_specs=[pl.BlockSpec(memory_space=pl.ANY)] * 7,
        out_specs=vmem,
        scratch_shapes=[
            pltpu.VMEM(continuum.shape, BF16),
            pltpu.VMEM(angle_weight.shape, F32),
            pltpu.VMEM((1, modes), jnp.int32),
            pltpu.VMEM((1, padded), jnp.int32),
            pltpu.SMEM(radius.shape, F32),
            pltpu.SMEM(radius.shape, F32),
            dma((6,)),
            pltpu.VMEM((modes, points), BF16),
            pltpu.VMEM((2, *occupied.shape), BF16),
            pltpu.VMEM((2, rows, wide), F32),
            pltpu.VMEM((4, wide), F32),
            pltpu.VMEM((2 * rows, wide), BF16),
            pltpu.VMEM((chunks, rows, CHUNK), F32),
            pltpu.VMEM((chunks, rows, CHUNK), F32),
            pltpu.VMEM((chunks, rows, CHUNK), F32),
            pltpu.VMEM((units, 2 * half, LANES), BF16),
            pltpu.VMEM((n_rad, 2 * half, LANES), BF16),
            pltpu.VMEM((n_rad, 2 * half, LANES), BF16),
            pltpu.VMEM((units, 2 * half, LANES), BF16),
            pltpu.VMEM((2 * rows, padded), BF16),
            dma,
            dma((2,)),
            dma((2,)),
            dma((chunks,)),
            dma((chunks,)),
            dma((units,)),
            dma((n_rad,)),
            dma((n_rad,)),
            dma((units,)),
        ],
        compiler_params=pltpu.CompilerParams(
            collective_id=0, has_side_effects=True, vmem_limit_bytes=63 * 1024 * 1024
        ),
        cost_estimate=pl.CostEstimate(
            flops=8 * rows * points * modes, bytes_accessed=2 * points * modes, transcendentals=0
        ),
    )(
        occupied, continuum, angle_weight, harmonic_order[None], radius, radial_weight,
        harmonics.T,
    )
    return field


def solution(mesh):
    placed = (
        P("orb", None, "rad", None),
        P(None, ("grp", "rad"), None),
        P("orb", None),
        P(),
        P("rad"),
        P("rad"),
        P(),
    )
    return jax.shard_map(
        on_device,
        mesh=mesh,
        in_specs=placed,
        out_specs=P(None, ("grp", "rad"), "orb"),
        check_vma=False,
    )
```
